256 devices in a mesh: rep: 64 (over y_lo, z, x), tp: 4 (over y_hi, core).
Axes of the slice: x: 4, y: 4 (y_hi: 2, y_lo: 2; y = y_hi * 2 + y_lo), z: 8, core: 2. Of those that a mesh axis runs over, the one named last changes fastest.
Arguments:
- hidden_in: bfloat16 [64, 512, 8192], P('rep', 'tp'), may hold values from -6 to 6
- queries: bfloat16 [64, 512, 4096], P('rep', None, 'tp'), may hold values from -110 to 110
- out_grad: bfloat16 [64, 512, 4096], P('rep', None, 'tp'), may hold values from -6 to 6
- token_ids: int32 [64, 512], P('rep'), may hold values from 0 to 128000, as said below
- key_weight: bfloat16 [64, 8192, 512], P('rep', None, 'tp'), may hold values from -6 to 6
- value_weight: bfloat16 [64, 8192, 512], P('rep', None, 'tp'), may hold values from -6 to 6
- push_weight: bfloat16 [64], P('rep'), may hold values from 0.5 to 2
- gossip: int32 [16], replicated, may hold values from 0 to 2
Outputs:
- new_key_weight: bfloat16 [64, 8192, 512], P('rep', None, 'tp')
- new_value_weight: bfloat16 [64, 8192, 512], P('rep', None, 'tp')
- new_push_weight: bfloat16 [64], P('rep')
The draws below stay inside these ranges and needn't reach their ends.
Inputs may be any that keep to these rules, and one draw needn't show every extreme that they name: `token_ids`: each replica's sequence begins with the id 128000, which marks the start of a document, and holds it at further positions now and then.
All inputs are finite; a program needn't handle non-finite values.
Results may differ from the reference program's by a relative error of at most 0.015.
The reference program's roundings to bfloat16 on the way (of `prob_bf` and `grad_s`) count: a program that leaves them out, or rounds other values in their place, can miss the bound.
Values may be sent and summed in bfloat16 or wider, within the bound.
A program may use at most 128 MiB of HBM per device.

```python
import math
import jax
import jax.numpy as jnp
from jax import lax

D = 8192
HS = 128
KVH = 4
GROUP = 8
LEVELS = 3
TOK_DEV = 128
SEQ = 512
QH = 32
N_REP = 64


def draw_queries(key, part):
    key = jax.random.fold_in(key, 11)
    first = jax.random.fold_in(key, 0)
    shape = (N_REP, SEQ, KVH * GROUP * HS)
    base = jnp.clip(jax.random.normal(first, shape, jnp.float32), -6.0, 6.0)
    return base.astype(jnp.bfloat16)


def draw_token_ids(key, part):
    key = jax.random.fold_in(key, 23)
    first, second = jax.random.split(key)
    drawn = jax.random.randint(first, (N_REP, SEQ), 0, 128000)
    starts = jax.random.randint(second, (N_REP, SEQ), 0, 2 * TOK_DEV) == 0
    starts = starts.at[:, 0].set(True)
    return jnp.where(starts, 128000, drawn).astype(jnp.int32)


def touch_ends(result, stream_key, low, top_value):
    place = [jax.random.randint(jax.random.fold_in(stream_key, axis), (), 0, length) for axis, length in enumerate(result.shape)]
    main_axis = result.shape.index(max(result.shape))
    next_to = place[:main_axis] + [(place[main_axis] + 1) % result.shape[main_axis]] + place[main_axis + 1:]
    return result.at[tuple(place)].set(low).at[tuple(next_to)].set(top_value)


def level_of(own_key, dims, shards, smallest, top_value):
    gain, own = 1.0, jax.random.fold_in(own_key, 6)
    for dim, shards_of in shards:
        steps = jnp.exp(jax.random.uniform(jax.random.fold_in(own, dim), (shards_of,), jnp.float32, smallest / len(shards), top_value / len(shards)))
        gain = gain * jnp.repeat(steps, dims[dim] // shards_of).reshape([-1 if axis == dim else 1 for axis in range(len(dims))])
    return gain


def gaussian(rng, shape, width, most, cuts=(), dtype=jnp.bfloat16):
    entries = jax.random.normal(rng, shape, jnp.float32) * width
    if len(cuts) > 0:
        entries = level_of(rng, shape, cuts, -0.22, 0.18) * entries
    return jnp.clip(entries, min=-most, max=most).astype(dtype)


def setup_inputs(seed: int = 0) -> dict:
    key_of = jax.random.split(jax.random.key(seed), 9)
    hidden_in = gaussian(key_of[0], (N_REP, SEQ, D), 1.0, 6.0, ((0, 64), (1, 4)))
    queries = draw_queries(jax.random.fold_in(key_of[8], 71), 0)
    out_grad = gaussian(key_of[2], (N_REP, SEQ, QH * HS), 1.0, 6.0, ((0, 64), (2, 4)))
    token_ids = draw_token_ids(jax.random.fold_in(key_of[8], 71), 0)
    key_weight = gaussian(key_of[4], (N_REP, D, KVH * HS), 1.0, 6.0, ((0, 64), (2, 4)))
    value_weight = gaussian(key_of[5], (N_REP, D, KVH * HS), 1.0, 6.0, ((0, 64), (2, 4)))
    push_weight = jnp.clip(jnp.exp(math.log(2.0) - 1.3862944 * jax.random.uniform(key_of[6], (N_REP,), jnp.float32) ** level_of(key_of[6], (N_REP,), ((0, 64),), -0.2, 0.2)), 0.5, 2.0).astype(jnp.bfloat16)
    gossip = touch_ends(jax.random.randint(key_of[7], (16,), 0, LEVELS), jax.random.fold_in(key_of[7], 1), 0, LEVELS - 1).astype(jnp.int32)
    return dict(hidden_in=hidden_in, queries=queries, out_grad=out_grad, token_ids=token_ids, key_weight=key_weight, value_weight=value_weight, push_weight=push_weight, gossip=gossip)


doc_start = 128000
learn_rate = 0.5
epsilon = 1e-06

def attend(hidden_rows, query_rows, grad_rows, id_rows, key_numer, value_numer, push_value):
    inverse = 1.0 / push_value.astype(jnp.float32)
    key_z = (key_numer.astype(jnp.float32) * inverse).astype(jnp.bfloat16)
    value_z = (value_numer.astype(jnp.float32) * inverse).astype(jnp.bfloat16)
    scale_model = 1.0 / math.sqrt(D)
    head_scale = 1.0 / math.sqrt(HS)
    key_rows = (jnp.dot(hidden_rows, key_z, preferred_element_type=jnp.float32) * scale_model).astype(jnp.bfloat16)
    value_rows = (jnp.dot(hidden_rows, value_z, preferred_element_type=jnp.float32) * scale_model).astype(jnp.bfloat16)
    query_heads = query_rows.reshape(SEQ, KVH, GROUP, HS).astype(jnp.float32)
    key_heads = key_rows.reshape(SEQ, KVH, HS).astype(jnp.float32)
    value_heads = value_rows.reshape(SEQ, KVH, HS).astype(jnp.float32)
    segment = jnp.cumsum((id_rows == doc_start).astype(jnp.int32))
    position = jnp.arange(SEQ)
    allowed = (position[None, :] <= position[:, None]) & (segment[None, :] == segment[:, None])
    scores = jnp.einsum('sngd,tnd->ngst', query_heads, key_heads) * head_scale
    scores = jnp.where(allowed[None, None], scores, -1e+30)
    top_score = lax.optimization_barrier(jnp.max(scores, axis=-1, keepdims=True))
    expo = jnp.exp(scores - top_score)
    prob = expo / lax.optimization_barrier(jnp.sum(expo, axis=-1, keepdims=True))
    prob_bf = prob.astype(jnp.bfloat16).astype(jnp.float32)
    outputs = jnp.einsum('ngst,tnd->sngd', prob_bf, value_heads)
    grad_out = grad_rows.reshape(SEQ, KVH, GROUP, HS).astype(jnp.float32)
    delta = lax.optimization_barrier(jnp.sum(grad_out * outputs, axis=-1))
    grad_p = jnp.einsum('sngd,tnd->ngst', grad_out, value_heads)
    grad_s = (prob * (grad_p - jnp.transpose(delta, (1, 2, 0))[..., None])).astype(jnp.bfloat16)
    grad_v = jnp.einsum('ngst,sngd->tnd', prob_bf, grad_out).astype(jnp.bfloat16)
    grad_k = (jnp.einsum('ngst,sngd->tnd', grad_s.astype(jnp.float32), query_heads) * head_scale).astype(jnp.bfloat16)
    grad_kw = jnp.dot(hidden_rows.T, grad_k.reshape(SEQ, KVH * HS), preferred_element_type=jnp.float32) * scale_model
    grad_vw = jnp.dot(hidden_rows.T, grad_v.reshape(SEQ, KVH * HS), preferred_element_type=jnp.float32) * scale_model
    squares = jnp.sum(grad_kw * grad_kw) + jnp.sum(grad_vw * grad_vw)
    factor = lax.rsqrt(squares / (2 * D * KVH * HS) + epsilon)
    return ((grad_kw * factor).astype(jnp.bfloat16), (grad_vw * factor).astype(jnp.bfloat16))

def reference(hidden_in, queries, out_grad, token_ids, key_weight, value_weight, push_weight, gossip):
    dir_k, dir_v = lax.map(lambda items: attend(*items), (hidden_in, queries, out_grad, token_ids, key_weight, value_weight, push_weight))
    distance = jnp.left_shift(jnp.int32(1), gossip[0])

    def mixed(numer, step):
        peer_numer = jnp.roll(numer, distance, axis=0).astype(jnp.float32)
        peer_step = jnp.roll(step, distance, axis=0).astype(jnp.float32)
        own = numer.astype(jnp.float32)
        return (0.5 * (own + peer_numer) - 0.5 * learn_rate * (step.astype(jnp.float32) + peer_step)).astype(jnp.bfloat16)
    peer_push = jnp.roll(push_weight, distance, axis=0).astype(jnp.float32)
    new_push = (0.5 * (push_weight.astype(jnp.float32) + peer_push)).astype(jnp.bfloat16)
    return (mixed(key_weight, dir_k), mixed(value_weight, dir_v), new_push)
```

```python
from functools import partial
import math

import jax
import jax.numpy as jnp
from jax import lax
from jax.experimental import pallas as pl
from jax.experimental.pallas import tpu as pltpu
from jax.sharding import PartitionSpec as P

D = 8192
HS = 128
KVH = 4
GROUP = 8
LEVELS = 3
TOK = 128
SEQ = 512
N_REP = 64

doc_start = 128000
learn_rate = 0.5
epsilon = 1e-06

MESH = pl.DeviceIdType.MESH
BF = jnp.bfloat16
F32 = jnp.float32
MIB = 1024 * 1024

COLS = 1024
N_IN = D // COLS
ROWS = 512
N_OUT = D // ROWS


def dot_nn(a, b):
    return lax.dot_general(a, b, (((1,), (0,)), ((), ())), preferred_element_type=F32)


def dot_nt(a, b):
    return lax.dot_general(a, b, (((1,), (1,)), ((), ())), preferred_element_type=F32)


def dot_tn(a, b):
    return lax.dot_general(a, b, (((0,), (0,)), ((), ())), preferred_element_type=F32)


def kernel(
    distance,
    hid, qin, gin, ids, kin, vin, push,
    out_k, out_v, out_push,
    hbuf, qbuf, gbuf, kw, vw, bias, zbuf, acc, krow, vrow, gk, gv, gpair, gw, sqacc,
    abuf, rbuf, ostk, ostv, sq_mine, sq_peer, push_mine, push_peer,
    load_sem, y2_send, y2_recv, fw_send, fw_recv, core_send, core_recv,
    sq_send, sq_recv, rep_send, rep_recv, push_send, push_recv, out_sem,
):
    rep = lax.axis_index("rep")
    tp = lax.axis_index("tp")
    half = tp // 2
    core = lax.rem(tp, 2)
    other_core = (rep, half * 2 + 1 - core)
    other_half = (rep, (1 - half) * 2 + core)
    diagonal = (rep, (1 - half) * 2 + 1 - core)
    target = (lax.rem(rep + distance, N_REP), tp)
    source = (lax.rem(rep + N_REP - distance, N_REP), tp)

    mine = pl.ds(pl.multiple_of(tp * TOK, TOK), TOK)
    theirs = pl.ds(pl.multiple_of(other_half[1] * TOK, TOK), TOK)

    def remote(src, dst, send, recv, device):
        return pltpu.make_async_remote_copy(
            src_ref=src, dst_ref=dst, send_sem=send, recv_sem=recv,
            device_id=device, device_id_type=MESH,
        )

    loads = [
        pltpu.make_async_copy(src, dst, load_sem.at[n])
        for n, (src, dst) in enumerate(
            [(kin, kw), (vin, vw), (hid, hbuf.at[mine]), (qin, qbuf), (gin, gbuf)]
        )
    ]
    for copy in loads:
        copy.start()

    barrier = pltpu.get_barrier_semaphore()
    for device in (other_core, other_half, diagonal, source):
        pl.semaphore_signal(barrier, inc=1, device_id=device, device_id_type=MESH)
    pl.semaphore_wait(barrier, 4)

    def across(i):
        cols = pl.ds(pl.multiple_of(i * COLS, COLS), COLS)
        return remote(
            hid.at[:, cols], hbuf.at[mine, cols], y2_send.at[i], y2_recv.at[i], other_half
        )

    def onward(i):
        cols = pl.ds(pl.multiple_of(i * COLS, COLS), COLS)
        return remote(
            hbuf.at[theirs, cols], hbuf.at[theirs, cols], fw_send.at[i], fw_recv.at[i], other_core
        )

    def start_across(i, carry):
        across(i).start()
        return carry

    lax.fori_loop(0, N_IN, start_across, 0)
    beside = remote(hid, hbuf.at[mine], core_send, core_recv, other_core)
    beside.start()
    push_f32 = push[0:1, 0:1].astype(F32)
    push_mine[...] = jnp.broadcast_to(push_f32, (8, 128))
    push_along = remote(push_mine, push_peer, push_send, push_recv, target)
    push_along.start()

    with jax.named_scope("mask"):
        down = lax.broadcasted_iota(jnp.int32, (SEQ, SEQ), 0)
        over = lax.broadcasted_iota(jnp.int32, (SEQ, SEQ), 1)
        starts = jnp.broadcast_to((ids[...] == doc_start).astype(F32), (8, SEQ)).astype(BF)
        upper = (down <= over).astype(F32).astype(BF)
        lower = (over <= down).astype(F32).astype(BF)
        seg_row = dot_nn(starts, upper)
        seg_col = dot_nt(lower, starts)
        allowed = (down <= over) & (seg_col[:, 0:1] == seg_row[0:1, :])
        bias[...] = jnp.where(allowed, 0.0, -1e30)

    acc[...] = jnp.zeros_like(acc)
    gk[...] = jnp.zeros_like(gk)
    gv[...] = jnp.zeros_like(gv)
    sqacc[...] = jnp.zeros_like(sqacc)
    inverse = 1.0 / push_f32
    for copy in loads:
        copy.wait()
    beside.wait()

    def project(i, carry):
        @pl.when(i < N_IN)
        def _():
            across(i).wait_recv()
            onward(i).start()

        @pl.when(i > 0)
        def _():
            j = i - 1
            onward(j).wait_recv()
            rows = pl.ds(pl.multiple_of(j * COLS, COLS), COLS)
            zbuf[:, 0:HS] = (kw[rows, :].astype(F32) * inverse).astype(BF)
            zbuf[:, HS:] = (vw[rows, :].astype(F32) * inverse).astype(BF)
            acc[...] += dot_nn(hbuf[:, rows], zbuf[...])

        return carry

    with jax.named_scope("project"):
        lax.fori_loop(0, N_IN + 1, project, 0)

    scale_model = 1.0 / math.sqrt(D)
    head_scale = 1.0 / math.sqrt(HS)
    krow[...] = (acc[:, 0:HS] * scale_model).astype(BF)
    vrow[...] = (acc[:, HS:] * scale_model).astype(BF)

    def head(g, carry):
        lanes = pl.ds(pl.multiple_of(g * HS, HS), HS)
        for first, count, keys in ((0, 256, 256), (256, 256, 512)):
            query = qbuf[first : first + count, lanes]
            grad = gbuf[first : first + count, lanes]
            scores = dot_nt(krow[0:keys, :], query) * head_scale
            scores = scores + bias[0:keys, first : first + count]
            grad_p = dot_nt(vrow[0:keys, :], grad)
            expo = jnp.exp(scores - jnp.max(scores, axis=0, keepdims=True))
            prob = expo * (1.0 / jnp.sum(expo, axis=0, keepdims=True))
            prob_bf = prob.astype(BF)
            delta = jnp.sum(prob_bf.astype(F32) * grad_p, axis=0, keepdims=True)
            grad_s = (prob * (grad_p - delta)).astype(BF)
            gv[0:keys, :] += dot_nn(prob_bf, grad)
            gk[0:keys, :] += dot_nn(grad_s, query)
        return carry

    with jax.named_scope("attend"):
        lax.fori_loop(0, GROUP, head, 0)
    gpair[:, 0:HS] = (gk[...] * head_scale).astype(BF)
    gpair[:, HS:] = gv[...].astype(BF)

    def weight_grad(i, carry):
        rows = pl.ds(pl.multiple_of(i * ROWS, ROWS), ROWS)
        g = dot_tn(hbuf[:, rows], gpair[...]) * scale_model
        gw[rows, :] = g
        sqacc[...] += jnp.sum((g * g).reshape(ROWS // 8, 8, 2 * HS), axis=0)
        return carry

    with jax.named_scope("weight_grad"):
        lax.fori_loop(0, N_OUT, weight_grad, 0)

    sq_mine[...] = jnp.broadcast_to(jnp.sum(sqacc[...], keepdims=True), (8, 128))
    shares = [
        remote(sq_mine, sq_peer.at[n], sq_send.at[n], sq_recv.at[n], device)
        for n, device in enumerate((other_core, other_half, diagonal))
    ]
    for copy in shares:
        copy.start()
    for copy in shares:
        copy.wait()
    squares = (sq_mine[0:1, 0:1] + sq_peer[0, 0:1, 0:1]) + (
        sq_peer[1, 0:1, 0:1] + sq_peer[2, 0:1, 0:1]
    )
    factor = lax.rsqrt(squares / (2 * D * KVH * HS) + epsilon)

    def own_part(rows):
        step = (gw[rows, :] * factor).astype(BF).astype(F32)
        own_k = 0.5 * kw[rows, :].astype(F32) - (0.5 * learn_rate) * step[:, 0:HS]
        own_v = 0.5 * vw[rows, :].astype(F32) - (0.5 * learn_rate) * step[:, HS:]
        return own_k, own_v

    def along(i):
        rows = pl.ds(pl.multiple_of(i * ROWS, ROWS), ROWS)
        return remote(abuf.at[rows], rbuf.at[rows], rep_send.at[i], rep_recv.at[i], target)

    def send_part(i, carry):
        rows = pl.ds(pl.multiple_of(i * ROWS, ROWS), ROWS)
        own_k, own_v = own_part(rows)
        abuf[rows, 0:HS] = own_k.astype(BF)
        abuf[rows, HS:] = own_v.astype(BF)
        along(i).start()
        return carry

    with jax.named_scope("send_parts"):
        lax.fori_loop(0, N_OUT, send_part, 0)

    push_along.wait()
    out_push[...] = (0.5 * (push_f32 + push_peer[0:1, 0:1])).astype(BF)

    def written(i):
        rows = pl.ds(pl.multiple_of(i * ROWS, ROWS), ROWS)
        return (
            pltpu.make_async_copy(ostk.at[rows], out_k.at[rows], out_sem.at[0, i]),
            pltpu.make_async_copy(ostv.at[rows], out_v.at[rows], out_sem.at[1, i]),
        )

    def mix(i, carry):
        rows = pl.ds(pl.multiple_of(i * ROWS, ROWS), ROWS)
        own_k, own_v = own_part(rows)
        along(i).wait_recv()
        ostk[rows, :] = (own_k + rbuf[rows, 0:HS].astype(F32)).astype(BF)
        ostv[rows, :] = (own_v + rbuf[rows, HS:].astype(F32)).astype(BF)
        for copy in written(i):
            copy.start()
        return carry

    with jax.named_scope("mix"):
        lax.fori_loop(0, N_OUT, mix, 0)

    def finish(i, carry):
        along(i).wait_send()
        for copy in written(i):
            copy.wait()
        return carry

    lax.fori_loop(0, N_OUT, finish, 0)

    def sent(i, carry):
        across(i).wait_send()
        onward(i).wait_send()
        return carry

    lax.fori_loop(0, N_IN, sent, 0)


def run(level, hid, qin, gin, ids, kin, vin, push):
    vmem = pltpu.VMEM
    dma = pltpu.SemaphoreType.DMA
    whole = pl.BlockSpec(memory_space=pltpu.VMEM)
    hbm = pl.BlockSpec(memory_space=pl.ANY)
    return pl.pallas_call(
        partial(kernel, 1 << level),
        name=f"gossip_step_{1 << level}",
        out_shape=(
            jax.ShapeDtypeStruct((D, HS), BF),
            jax.ShapeDtypeStruct((D, HS), BF),
            jax.ShapeDtypeStruct((1, 1), BF),
        ),
        in_specs=[hbm, hbm, hbm, whole, hbm, hbm, whole],
        out_specs=(hbm, hbm, whole),
        scratch_shapes=[
            vmem((SEQ, D), BF),
            vmem((SEQ, GROUP * HS), BF),
            vmem((SEQ, GROUP * HS), BF),
            vmem((D, HS), BF),
            vmem((D, HS), BF),
            vmem((SEQ, SEQ), F32),
            vmem((COLS, 2 * HS), BF),
            vmem((SEQ, 2 * HS), F32),
            vmem((SEQ, HS), BF),
            vmem((SEQ, HS), BF),
            vmem((SEQ, HS), F32),
            vmem((SEQ, HS), F32),
            vmem((SEQ, 2 * HS), BF),
            vmem((D, 2 * HS), F32),
            vmem((8, 2 * HS), F32),
            vmem((D, 2 * HS), BF),
            vmem((D, 2 * HS), BF),
            vmem((D, HS), BF),
            vmem((D, HS), BF),
            vmem((8, 128), F32),
            vmem((3, 8, 128), F32),
            vmem((8, 128), F32),
            vmem((8, 128), F32),
            dma((5,)),
            dma((N_IN,)),
            dma((N_IN,)),
            dma((N_IN,)),
            dma((N_IN,)),
            dma,
            dma,
            dma((3,)),
            dma((3,)),
            dma((N_OUT,)),
            dma((N_OUT,)),
            dma,
            dma,
            dma((2, N_OUT)),
        ],
        compiler_params=pltpu.CompilerParams(
            collective_id=level, has_side_effects=True, vmem_limit_bytes=58 * MIB
        ),
        cost_estimate=pl.CostEstimate(
            flops=7_000_000_000, bytes_accessed=16 * MIB, transcendentals=2_000_000
        ),
    )(hid, qin, gin, ids, kin, vin, push)


def body(hidden_in, queries, out_grad, token_ids, key_weight, value_weight, push_weight, gossip):
    args = (
        hidden_in[0], queries[0], out_grad[0], token_ids, key_weight[0], value_weight[0],
        push_weight.reshape(1, 1),
    )
    new_key, new_value, new_push = lax.switch(
        gossip[0], [partial(run, level) for level in range(LEVELS)], *args
    )
    return new_key[None], new_value[None], new_push.reshape(1)


def solution(mesh):
    return jax.shard_map(
        body,
        mesh=mesh,
        in_specs=(
            P("rep", "tp", None),
            P("rep", None, "tp"),
            P("rep", None, "tp"),
            P("rep", None),
            P("rep", None, "tp"),
            P("rep", None, "tp"),
            P("rep"),
            P(),
        ),
        out_specs=(P("rep", None, "tp"), P("rep", None, "tp"), P("rep")),
        check_vma=False,
    )
```

```python
from functools import partial
import math

import jax
import jax.numpy as jnp
from jax import lax
from jax.experimental import pallas as pl
from jax.experimental.pallas import tpu as pltpu
from jax.sharding import PartitionSpec as P

D = 8192
HS = 128
KVH = 4
GROUP = 8
LEVELS = 3
TOK = 128
SEQ = 512
N_REP = 64

doc_start = 128000
learn_rate = 0.5
epsilon = 1e-06

MESH = pl.DeviceIdType.MESH
BF = jnp.bfloat16
F32 = jnp.float32
MIB = 1024 * 1024

COLS = 512
N_IN = D // COLS
ROWS = 256
N_OUT = D // ROWS
BLOCK = 128
N_BLOCK = SEQ // BLOCK
SPAN = 1
WIDE = 1024


def dot_nn(a, b):
    return lax.dot_general(a, b, (((1,), (0,)), ((), ())), preferred_element_type=F32)


def dot_nt(a, b):
    return lax.dot_general(a, b, (((1,), (1,)), ((), ())), preferred_element_type=F32)


def dot_tn(a, b):
    return lax.dot_general(a, b, (((0,), (0,)), ((), ())), preferred_element_type=F32)


def kernel(
    distance,
    hid, qin, gin, ids, kin, vin, push,
    out_k, out_v, out_push,
    hbuf, qbuf, gbuf, kw, vw, bias, zbuf, acc, krow, vrow, gk, gv, gpair, gw,
    abuf, rbuf, ostk, ostv, gram,
    sq_mine, sq_peer, push_mine, push_peer,
    load_sem, y2_send, y2_recv, fw_send, fw_recv, core_send, core_recv,
    sq_send, sq_recv, rep_send, rep_recv, push_send, push_recv,
    credit, head_sem, out_sem,
):
    rep = lax.axis_index("rep")
    tp = lax.axis_index("tp")
    half = tp // 2
    core = lax.rem(tp, 2)
    other_core = (rep, half * 2 + 1 - core)
    other_half = (rep, (1 - half) * 2 + core)
    diagonal = (rep, (1 - half) * 2 + 1 - core)
    target = (lax.rem(rep + distance, N_REP), tp)
    source = (lax.rem(rep + N_REP - distance, N_REP), tp)

    mine = pl.ds(pl.multiple_of(tp * TOK, TOK), TOK)
    theirs = pl.ds(pl.multiple_of(other_half[1] * TOK, TOK), TOK)

    def remote(src, dst, send, recv, device):
        return pltpu.make_async_remote_copy(
            src_ref=src, dst_ref=dst, send_sem=send, recv_sem=recv,
            device_id=device, device_id_type=MESH,
        )

    loads = [
        pltpu.make_async_copy(src, dst, load_sem.at[n])
        for n, (src, dst) in enumerate(
            [(kin, kw), (vin, vw), (hid, hbuf.at[mine])]
        )
    ]
    head_loads = [
        pltpu.make_async_copy(
            src.at[:, :, pl.ds(g * HS, HS)],
            dst.at[:, pl.ds(g * BLOCK, BLOCK), :],
            head_sem.at[n, g],
        )
        for n, (src, dst) in enumerate([(qin, qbuf), (gin, gbuf)])
        for g in range(GROUP)
    ]
    for copy in loads:
        copy.start()

    barrier = pltpu.get_barrier_semaphore()
    for device in (other_core, other_half, diagonal, source):
        pl.semaphore_signal(barrier, inc=1, device_id=device, device_id_type=MESH)
    pl.semaphore_wait(barrier, 4)

    def across(i):
        cols = pl.ds(pl.multiple_of(i * COLS, COLS), COLS)
        return remote(
            hid.at[:, cols], hbuf.at[mine, cols], y2_send.at[i], y2_recv.at[i], other_half
        )

    def onward(i):
        cols = pl.ds(pl.multiple_of(i * COLS, COLS), COLS)
        return remote(
            hbuf.at[theirs, cols], hbuf.at[theirs, cols], fw_send.at[i], fw_recv.at[i], other_core
        )

    def start_across(i, carry):
        across(i).start()
        return carry

    lax.fori_loop(0, N_IN, start_across, 0)
    beside = remote(hid, hbuf.at[mine], core_send, core_recv, other_core)
    beside.start()
    push_f32 = push[0:1, 0:1].astype(F32)
    push_mine[...] = jnp.broadcast_to(push_f32, (8, 128))
    push_along = remote(push_mine, push_peer, push_send, push_recv, target)
    push_along.start()
    for copy in head_loads:
        copy.start()

    with jax.named_scope("mask"):
        down = lax.broadcasted_iota(jnp.int32, (SEQ, SEQ), 0)
        over = lax.broadcasted_iota(jnp.int32, (SEQ, SEQ), 1)
        starts = jnp.broadcast_to((ids[...] == doc_start).astype(F32), (8, SEQ)).astype(BF)
        upper = (down <= over).astype(F32).astype(BF)
        lower = (over <= down).astype(F32).astype(BF)
        seg_row = dot_nn(starts, upper)
        seg_col = dot_nt(lower, starts)
        allowed = (down <= over) & (seg_col[:, 0:1] == seg_row[0:1, :])
        bias[...] = jnp.where(allowed, 0.0, -1e30)

    acc[...] = jnp.zeros_like(acc)
    gk[...] = jnp.zeros_like(gk)
    gv[...] = jnp.zeros_like(gv)
    gram[...] = jnp.zeros_like(gram)
    inverse = 1.0 / push_f32
    for copy in loads:
        copy.wait()
    beside.wait()

    def project(i, carry):
        @pl.when(i < N_IN)
        def _():
            across(i).wait_recv()
            onward(i).start()

        @pl.when(i > 0)
        def _():
            j = i - 1
            onward(j).wait_recv()
            rows = pl.ds(pl.multiple_of(j * COLS, COLS), COLS)
            zbuf[:, 0:HS] = (kw[rows, :].astype(F32) * inverse).astype(BF)
            zbuf[:, HS:] = (vw[rows, :].astype(F32) * inverse).astype(BF)
            part = hbuf[:, rows]
            acc[...] += dot_nn(part, zbuf[...])
            gram[...] += dot_nt(part, part)

        return carry

    with jax.named_scope("project"):
        lax.fori_loop(0, N_IN + 1, project, 0)

    scale_model = 1.0 / math.sqrt(D)
    head_scale = 1.0 / math.sqrt(HS)
    krow[...] = (acc[:, 0:HS] * scale_model).astype(BF)
    vrow[...] = (acc[:, HS:] * scale_model).astype(BF)

    for copy in head_loads:
        copy.wait()

    def attend(keys, query, grad, mask):
        scores = dot_nt(krow[0:keys, :], query) * (head_scale * math.log2(math.e))
        scores = scores + jnp.concatenate([mask] * (query.shape[0] // BLOCK), axis=1)
        expo = jnp.exp2(scores - jnp.max(scores, axis=0, keepdims=True))
        grad_p = dot_nt(vrow[0:keys, :], grad)
        prob = expo * (1.0 / jnp.sum(expo, axis=0, keepdims=True))
        prob_bf = prob.astype(BF)
        delta = jnp.sum(prob_bf.astype(F32) * grad_p, axis=0, keepdims=True)
        grad_s = (prob * (grad_p - delta)).astype(BF)
        gv[0:keys, :] += dot_nn(prob_bf, grad)
        gk[0:keys, :] += dot_nn(grad_s, query)

    def attend_step(first, keys, n, carry):
        per_block = GROUP * BLOCK // WIDE
        block = first + n // per_block
        rows = pl.ds(pl.multiple_of(lax.rem(n, per_block) * WIDE, WIDE), WIDE)
        lanes = pl.ds(pl.multiple_of(block * BLOCK, BLOCK), BLOCK)
        attend(keys, qbuf[block, rows, :], gbuf[block, rows, :], bias[0:keys, lanes])
        return carry

    with jax.named_scope("attend"):
        for first in range(0, N_BLOCK, SPAN):
            lax.fori_loop(
                0,
                SPAN * GROUP * BLOCK // WIDE,
                partial(attend_step, first, (first + SPAN) * BLOCK),
                0,
            )
    gpair[:, 0:HS] = (gk[...] * head_scale).astype(BF)
    gpair[:, HS:] = gv[...].astype(BF)

    with jax.named_scope("squares"):
        pair = gpair[...]
        high = gram[...].astype(BF)
        rest = gram[...] - high.astype(F32)
        middle = rest.astype(BF)
        low = (rest - middle.astype(F32)).astype(BF)
        spread = dot_nn(low, pair) + dot_nn(middle, pair) + dot_nn(high, pair)
        total = jnp.sum(spread * pair.astype(F32), keepdims=True)
        sq_mine[...] = jnp.broadcast_to(
            jnp.maximum(total, 0.0) * (scale_model * scale_model), (8, 128)
        )
    shares = [
        remote(sq_mine, sq_peer.at[n], sq_send.at[n], sq_recv.at[n], device)
        for n, device in enumerate((other_core, other_half, diagonal))
    ]
    for copy in shares:
        copy.start()

    def weight_grad(i):
        rows = pl.ds(pl.multiple_of(i * ROWS, ROWS), ROWS)
        gw[rows, :] = dot_tn(hbuf[:, rows], gpair[...]) * scale_model

    weight_grad(0)
    push_along.wait()
    for copy in shares:
        copy.wait()
    squares = (sq_mine[0:1, 0:1] + sq_peer[0, 0:1, 0:1]) + (
        sq_peer[1, 0:1, 0:1] + sq_peer[2, 0:1, 0:1]
    )
    factor = lax.rsqrt(squares / (2 * D * KVH * HS) + epsilon)
    pl.semaphore_signal(credit, inc=1, device_id=source, device_id_type=MESH)

    def own_part(rows):
        step = (gw[rows, :] * factor).astype(BF).astype(F32)
        own_k = 0.5 * kw[rows, :].astype(F32) - (0.5 * learn_rate) * step[:, 0:HS]
        own_v = 0.5 * vw[rows, :].astype(F32) - (0.5 * learn_rate) * step[:, HS:]
        return own_k, own_v

    def along(i):
        rows = pl.ds(pl.multiple_of(i * ROWS, ROWS), ROWS)
        return remote(abuf.at[rows], rbuf.at[rows], rep_send.at[i], rep_recv.at[i], target)

    def send_part(i, carry):
        rows = pl.ds(pl.multiple_of(i * ROWS, ROWS), ROWS)
        own_k, own_v = own_part(rows)
        abuf[rows, 0:HS] = own_k.astype(BF)
        abuf[rows, HS:] = own_v.astype(BF)

        @pl.when(i == 0)
        def _():
            pl.semaphore_wait(credit, 1)

        along(i).start()

        @pl.when(i + 1 < N_OUT)
        def _():
            weight_grad(i + 1)

        return carry

    with jax.named_scope("send_parts"):
        lax.fori_loop(0, N_OUT, send_part, 0)

    out_push[...] = (0.5 * (push_f32 + push_peer[0:1, 0:1])).astype(BF)

    def written(i):
        rows = pl.ds(pl.multiple_of(i * ROWS, ROWS), ROWS)
        return (
            pltpu.make_async_copy(ostk.at[rows], out_k.at[rows], out_sem.at[0, i]),
            pltpu.make_async_copy(ostv.at[rows], out_v.at[rows], out_sem.at[1, i]),
        )

    def mix(i, carry):
        rows = pl.ds(pl.multiple_of(i * ROWS, ROWS), ROWS)
        own_k, own_v = own_part(rows)
        along(i).wait_recv()
        ostk[rows, :] = (own_k + rbuf[rows, 0:HS].astype(F32)).astype(BF)
        ostv[rows, :] = (own_v + rbuf[rows, HS:].astype(F32)).astype(BF)
        for copy in written(i):
            copy.start()
        return carry

    with jax.named_scope("mix"):
        lax.fori_loop(0, N_OUT, mix, 0)

    def finish(i, carry):
        along(i).wait_send()
        for copy in written(i):
            copy.wait()
        return carry

    lax.fori_loop(0, N_OUT, finish, 0)

    def sent(i, carry):
        across(i).wait_send()
        onward(i).wait_send()
        return carry

    lax.fori_loop(0, N_IN, sent, 0)


def run(level, hid, qin, gin, ids, kin, vin, push):
    vmem = pltpu.VMEM
    dma = pltpu.SemaphoreType.DMA
    whole = pl.BlockSpec(memory_space=pltpu.VMEM)
    hbm = pl.BlockSpec(memory_space=pl.ANY)
    return pl.pallas_call(
        partial(kernel, 1 << level),
        name=f"gossip_step_{1 << level}",
        out_shape=(
            jax.ShapeDtypeStruct((D, HS), BF),
            jax.ShapeDtypeStruct((D, HS), BF),
            jax.ShapeDtypeStruct((1, 1), BF),
        ),
        in_specs=[hbm, hbm, hbm, whole, hbm, hbm, whole],
        out_specs=(hbm, hbm, whole),
        scratch_shapes=[
            vmem((SEQ, D), BF),
            vmem((N_BLOCK, GROUP * BLOCK, HS), BF),
            vmem((N_BLOCK, GROUP * BLOCK, HS), BF),
            vmem((D, HS), BF),
            vmem((D, HS), BF),
            vmem((SEQ, SEQ), F32),
            vmem((COLS, 2 * HS), BF),
            vmem((SEQ, 2 * HS), F32),
            vmem((SEQ, HS), BF),
            vmem((SEQ, HS), BF),
            vmem((SEQ, HS), F32),
            vmem((SEQ, HS), F32),
            vmem((SEQ, 2 * HS), BF),
            vmem((D, 2 * HS), F32),
            vmem((D, 2 * HS), BF),
            vmem((D, 2 * HS), BF),
            vmem((D, HS), BF),
            vmem((D, HS), BF),
            vmem((SEQ, SEQ), F32),
            vmem((8, 128), F32),
            vmem((3, 8, 128), F32),
            vmem((8, 128), F32),
            vmem((8, 128), F32),
            dma((3,)),
            dma((N_IN,)),
            dma((N_IN,)),
            dma((N_IN,)),
            dma((N_IN,)),
            dma,
            dma,
            dma((3,)),
            dma((3,)),
            dma((N_OUT,)),
            dma((N_OUT,)),
            dma,
            dma,
            pltpu.SemaphoreType.REGULAR,
            dma((2, GROUP)),
            dma((2, N_OUT)),
        ],
        compiler_params=pltpu.CompilerParams(
            collective_id=level, has_side_effects=True, vmem_limit_bytes=58 * MIB
        ),
        cost_estimate=pl.CostEstimate(
            flops=7_000_000_000, bytes_accessed=16 * MIB, transcendentals=2_000_000
        ),
    )(hid, qin, gin, ids, kin, vin, push)


def body(hidden_in, queries, out_grad, token_ids, key_weight, value_weight, push_weight, gossip):
    args = (
        hidden_in[0], queries.reshape(N_BLOCK, BLOCK, GROUP * HS),
        out_grad.reshape(N_BLOCK, BLOCK, GROUP * HS), token_ids, key_weight[0],
        value_weight[0], push_weight.reshape(1, 1),
    )
    new_key, new_value, new_push = lax.switch(
        gossip[0], [partial(run, level) for level in range(LEVELS)], *args
    )
    return new_key[None], new_value[None], new_push.reshape(1)


def solution(mesh):
    return jax.shard_map(
        body,
        mesh=mesh,
        in_specs=(
            P("rep", "tp", None),
            P("rep", None, "tp"),
            P("rep", None, "tp"),
            P("rep", None),
            P("rep", None, "tp"),
            P("rep", None, "tp"),
            P("rep"),
            P(),
        ),
        out_specs=(P("rep", None, "tp"), P("rep", None, "tp"), P("rep")),
        check_vma=False,
    )
```

```python
from functools import partial
import math

import jax
import jax.numpy as jnp
from jax import lax
from jax.experimental import pallas as pl
from jax.experimental.pallas import tpu as pltpu
from jax.sharding import PartitionSpec as P

D = 8192
HS = 128
KVH = 4
GROUP = 8
LEVELS = 3
TOK = 128
SEQ = 512
N_REP = 64

doc_start = 128000
learn_rate = 0.5
epsilon = 1e-06

MESH = pl.DeviceIdType.MESH
BF = jnp.bfloat16
F32 = jnp.float32
MIB = 1024 * 1024

COLS = 512
N_IN = D // COLS
ROWS = 512
N_OUT = D // ROWS
BLOCK = 128
N_BLOCK = SEQ // BLOCK
SPAN = 2
WIDE = 1024


def dot_nn(a, b):
    return lax.dot_general(a, b, (((1,), (0,)), ((), ())), preferred_element_type=F32)


def dot_nt(a, b):
    return lax.dot_general(a, b, (((1,), (1,)), ((), ())), preferred_element_type=F32)


def dot_tn(a, b):
    return lax.dot_general(a, b, (((0,), (0,)), ((), ())), preferred_element_type=F32)


def kernel(
    distance,
    hid, qin, gin, ids, kin, vin, push,
    out_k, out_v, out_push,
    hbuf, qbuf, gbuf, kw, vw, bias, zbuf, acc, krow, vrow, gk, gv, gpair, gw,
    abuf, rbuf, ostk, ostv, gram, kw_peer, vw_peer, starts, seg_row,
    sq_mine, sq_peer, push_mine, push_peer, factor_mine, factor_peer,
    load_sem, y2_send, y2_recv, fw_send, fw_recv, core_send, core_recv,
    sq_send, sq_recv, rep_send, rep_recv, push_send, push_recv,
    factor_send, factor_recv, ahead_send, ahead_recv, credit, head_sem, out_sem,
):
    rep = lax.axis_index("rep")
    tp = lax.axis_index("tp")
    half = tp // 2
    core = lax.rem(tp, 2)
    other_core = (rep, half * 2 + 1 - core)
    other_half = (rep, (1 - half) * 2 + core)
    diagonal = (rep, (1 - half) * 2 + 1 - core)
    target = (lax.rem(rep + distance, N_REP), tp)
    source = (lax.rem(rep + N_REP - distance, N_REP), tp)

    mine = pl.ds(pl.multiple_of(tp * TOK, TOK), TOK)
    theirs = pl.ds(pl.multiple_of(other_half[1] * TOK, TOK), TOK)

    def remote(src, dst, send, recv, device):
        return pltpu.make_async_remote_copy(
            src_ref=src, dst_ref=dst, send_sem=send, recv_sem=recv,
            device_id=device, device_id_type=MESH,
        )

    loads = [
        pltpu.make_async_copy(src, dst, load_sem.at[n])
        for n, (src, dst) in enumerate(
            [(kin, kw), (vin, vw), (hid, hbuf.at[mine])]
        )
    ]
    head_loads = [
        pltpu.make_async_copy(
            src.at[:, :, pl.ds(g * HS, HS)],
            dst.at[:, pl.ds(g * BLOCK, BLOCK), :],
            head_sem.at[n, g],
        )
        for n, (src, dst) in enumerate([(qin, qbuf), (gin, gbuf)])
        for g in range(GROUP)
    ]
    for copy in loads:
        copy.start()

    barrier = pltpu.get_barrier_semaphore()
    for device in (other_core, other_half, diagonal, source):
        pl.semaphore_signal(barrier, inc=1, device_id=device, device_id_type=MESH)
    pl.semaphore_wait(barrier, 4)

    def across(i):
        cols = pl.ds(pl.multiple_of(i * COLS, COLS), COLS)
        return remote(
            hid.at[:, cols], hbuf.at[mine, cols], y2_send.at[i], y2_recv.at[i], other_half
        )

    def onward(i):
        cols = pl.ds(pl.multiple_of(i * COLS, COLS), COLS)
        return remote(
            hbuf.at[theirs, cols], hbuf.at[theirs, cols], fw_send.at[i], fw_recv.at[i], other_core
        )

    def start_across(i, carry):
        across(i).start()
        return carry

    lax.fori_loop(0, N_IN, start_across, 0)
    beside = remote(hid, hbuf.at[mine], core_send, core_recv, other_core)
    beside.start()
    push_f32 = push[0:1, 0:1].astype(F32)
    push_mine[...] = jnp.broadcast_to(push_f32, (8, 128))
    push_along = remote(push_mine, push_peer, push_send, push_recv, target)
    push_along.start()
    for copy in head_loads:
        copy.start()

    with jax.named_scope("mask"):
        starts[...] = jnp.broadcast_to((ids[...] == doc_start).astype(F32), (16, SEQ)).astype(BF)
        seg_row[...] = jnp.zeros_like(seg_row)
        down = lax.broadcasted_iota(jnp.int32, (BLOCK, SEQ), 0)
        over = lax.broadcasted_iota(jnp.int32, (BLOCK, SEQ), 1)

        def add_row(n, carry):
            first = pl.multiple_of(n * BLOCK, BLOCK)
            upper = (down + first <= over).astype(F32).astype(BF)
            seg_row[...] += dot_nn(starts[:, pl.ds(first, BLOCK)], upper)
            return carry

        lax.fori_loop(0, N_BLOCK, add_row, 0)

        def mask_rows(n, carry):
            first = pl.multiple_of(n * BLOCK, BLOCK)
            lower = (over <= down + first).astype(F32).astype(BF)
            seg_col = dot_nt(lower, starts[...])
            allowed = (down + first <= over) & (seg_col[:, 0:1] == seg_row[0:1, :])
            bias[pl.ds(first, BLOCK), :] = jnp.where(allowed, 0.0, -1e30)
            return carry

        lax.fori_loop(0, N_BLOCK, mask_rows, 0)

    acc[...] = jnp.zeros_like(acc)
    gk[...] = jnp.zeros_like(gk)
    gv[...] = jnp.zeros_like(gv)
    gram[...] = jnp.zeros_like(gram)
    inverse = 1.0 / push_f32
    for copy in loads:
        copy.wait()
    beside.wait()

    def project(i, carry):
        @pl.when(i < N_IN)
        def _():
            across(i).wait_recv()
            onward(i).start()

        @pl.when(i > 0)
        def _():
            j = i - 1
            onward(j).wait_recv()
            rows = pl.ds(pl.multiple_of(j * COLS, COLS), COLS)
            zbuf[:, 0:HS] = (kw[rows, :].astype(F32) * inverse).astype(BF)
            zbuf[:, HS:] = (vw[rows, :].astype(F32) * inverse).astype(BF)
            part = hbuf[:, rows]
            acc[...] += dot_nn(part, zbuf[...])
            gram[...] += dot_nt(part, part)

        return carry

    with jax.named_scope("project"):
        lax.fori_loop(0, N_IN + 1, project, 0)

    ahead = [
        remote(src.at[pl.ds(0, ROWS)], dst, ahead_send.at[n], ahead_recv.at[n], target)
        for n, (src, dst) in enumerate([(kin, kw_peer), (vin, vw_peer)])
    ]
    for copy in ahead:
        copy.start()

    scale_model = 1.0 / math.sqrt(D)
    head_scale = 1.0 / math.sqrt(HS)
    krow[...] = (acc[:, 0:HS] * scale_model).astype(BF)
    vrow[...] = (acc[:, HS:] * scale_model).astype(BF)

    for copy in head_loads:
        copy.wait()

    def attend(keys, query, grad, mask):
        scores = dot_nt(krow[0:keys, :], query) * (head_scale * math.log2(math.e))
        scores = scores + jnp.concatenate([mask] * (query.shape[0] // BLOCK), axis=1)
        expo = jnp.exp2(scores - jnp.max(scores, axis=0, keepdims=True))
        grad_p = dot_nt(vrow[0:keys, :], grad)
        prob = expo * (1.0 / jnp.sum(expo, axis=0, keepdims=True))
        prob_bf = prob.astype(BF)
        delta = jnp.sum(prob_bf.astype(F32) * grad_p, axis=0, keepdims=True)
        grad_s = (prob * (grad_p - delta)).astype(BF)
        gv[0:keys, :] += dot_nn(prob_bf, grad)
        gk[0:keys, :] += dot_nn(grad_s, query)

    def attend_step(first, keys, n, carry):
        per_block = GROUP * BLOCK // WIDE
        block = first + n // per_block
        rows = pl.ds(pl.multiple_of(lax.rem(n, per_block) * WIDE, WIDE), WIDE)
        lanes = pl.ds(pl.multiple_of(block * BLOCK, BLOCK), BLOCK)
        attend(keys, qbuf[block, rows, :], gbuf[block, rows, :], bias[0:keys, lanes])
        return carry

    with jax.named_scope("attend"):
        for first in range(0, N_BLOCK, SPAN):
            lax.fori_loop(
                0,
                SPAN * GROUP * BLOCK // WIDE,
                partial(attend_step, first, (first + SPAN) * BLOCK),
                0,
            )
    gpair[:, 0:HS] = (gk[...] * head_scale).astype(BF)
    gpair[:, HS:] = gv[...].astype(BF)

    def weight_grad(i):
        rows = pl.ds(pl.multiple_of(i * ROWS, ROWS), ROWS)
        gw[rows, :] = dot_tn(hbuf[:, rows], gpair[...]) * scale_model

    def along(i):
        rows = pl.ds(pl.multiple_of(i * ROWS, ROWS), ROWS)
        return remote(abuf.at[rows], rbuf.at[rows], rep_send.at[i], rep_recv.at[i], target)

    shares = [
        remote(sq_mine, sq_peer.at[n], sq_send.at[n], sq_recv.at[n], device)
        for n, device in enumerate((other_core, other_half, diagonal))
    ]
    factor_along = remote(factor_mine, factor_peer, factor_send, factor_recv, target)

    def share_squares():
        def add_rows(n, total):
            rows = pl.ds(pl.multiple_of(n * 256, 256), 256)
            pair = gpair[...]
            whole = gram[rows, :]
            high = whole.astype(BF)
            rest = whole - high.astype(F32)
            middle = rest.astype(BF)
            low = (rest - middle.astype(F32)).astype(BF)
            spread = dot_nn(low, pair) + dot_nn(middle, pair) + dot_nn(high, pair)
            return total + jnp.sum(spread * gpair[rows, :].astype(F32), axis=0, keepdims=True)

        total = lax.fori_loop(0, SEQ // 256, add_rows, jnp.zeros((1, 2 * HS), F32))
        total = jnp.maximum(jnp.sum(total, keepdims=True), 0.0) * (scale_model * scale_model)
        sq_mine[...] = jnp.broadcast_to(total, (8, 128))
        for copy in shares:
            copy.start()

    def settle_factor():
        push_along.wait()
        for copy in shares:
            copy.wait()
        squares = (sq_mine[...] + sq_peer[0]) + (sq_peer[1] + sq_peer[2])
        factor_mine[...] = lax.rsqrt(squares / (2 * D * KVH * HS) + epsilon)
        pl.semaphore_signal(credit, inc=1, device_id=source, device_id_type=MESH)
        factor_along.start()
        pl.semaphore_wait(credit, 1)

    def own_part(rows):
        step = (gw[rows, :] * factor_mine[0:1, 0:1]).astype(BF).astype(F32)
        own_k = 0.5 * kw[rows, :].astype(F32) - (0.5 * learn_rate) * step[:, 0:HS]
        own_v = 0.5 * vw[rows, :].astype(F32) - (0.5 * learn_rate) * step[:, HS:]
        return own_k, own_v

    def send_part(i, carry):
        rows = pl.ds(pl.multiple_of(i * ROWS, ROWS), ROWS)
        weight_grad(i)

        @pl.when(i == 0)
        def _():
            abuf[rows, :] = gw[rows, :].astype(BF)
            along(i).start()
            share_squares()

        @pl.when(i == 1)
        def _():
            settle_factor()

        @pl.when(i > 0)
        def _():
            own_k, own_v = own_part(rows)
            abuf[rows, 0:HS] = own_k.astype(BF)
            abuf[rows, HS:] = own_v.astype(BF)
            along(i).start()

        return carry

    with jax.named_scope("send_parts"):
        lax.fori_loop(0, N_OUT, send_part, 0)

    out_push[...] = (0.5 * (push_f32 + push_peer[0:1, 0:1])).astype(BF)

    def written(i):
        rows = pl.ds(pl.multiple_of(i * ROWS, ROWS), ROWS)
        return (
            pltpu.make_async_copy(ostk.at[rows], out_k.at[rows], out_sem.at[0, i]),
            pltpu.make_async_copy(ostv.at[rows], out_v.at[rows], out_sem.at[1, i]),
        )

    def mix(i, carry):
        rows = pl.ds(pl.multiple_of(i * ROWS, ROWS), ROWS)
        own_k, own_v = own_part(rows)
        along(i).wait_recv()

        @pl.when(i == 0)
        def _():
            step = (rbuf[rows, :].astype(F32) * factor_peer[0:1, 0:1]).astype(BF).astype(F32)
            peer_k = 0.5 * kw_peer[...].astype(F32) - (0.5 * learn_rate) * step[:, 0:HS]
            peer_v = 0.5 * vw_peer[...].astype(F32) - (0.5 * learn_rate) * step[:, HS:]
            ostk[rows, :] = (own_k + peer_k).astype(BF)
            ostv[rows, :] = (own_v + peer_v).astype(BF)

        @pl.when(i > 0)
        def _():
            ostk[rows, :] = (own_k + rbuf[rows, 0:HS].astype(F32)).astype(BF)
            ostv[rows, :] = (own_v + rbuf[rows, HS:].astype(F32)).astype(BF)

        for copy in written(i):
            copy.start()
        return carry

    factor_along.wait()
    for copy in ahead:
        copy.wait()
    with jax.named_scope("mix"):
        lax.fori_loop(0, N_OUT, mix, 0)

    def finish(i, carry):
        along(i).wait_send()
        for copy in written(i):
            copy.wait()
        return carry

    lax.fori_loop(0, N_OUT, finish, 0)

    def sent(i, carry):
        across(i).wait_send()
        onward(i).wait_send()
        return carry

    lax.fori_loop(0, N_IN, sent, 0)


def run(level, hid, qin, gin, ids, kin, vin, push):
    vmem = pltpu.VMEM
    dma = pltpu.SemaphoreType.DMA
    whole = pl.BlockSpec(memory_space=pltpu.VMEM)
    hbm = pl.BlockSpec(memory_space=pl.ANY)
    return pl.pallas_call(
        partial(kernel, 1 << level),
        name=f"gossip_step_{1 << level}",
        out_shape=(
            jax.ShapeDtypeStruct((D, HS), BF),
            jax.ShapeDtypeStruct((D, HS), BF),
            jax.ShapeDtypeStruct((1, 1), BF),
        ),
        in_specs=[hbm, hbm, hbm, whole, hbm, hbm, whole],
        out_specs=(hbm, hbm, whole),
        scratch_shapes=[
            vmem((SEQ, D), BF),
            vmem((N_BLOCK, GROUP * BLOCK, HS), BF),
            vmem((N_BLOCK, GROUP * BLOCK, HS), BF),
            vmem((D, HS), BF),
            vmem((D, HS), BF),
            vmem((SEQ, SEQ), F32),
            vmem((COLS, 2 * HS), BF),
            vmem((SEQ, 2 * HS), F32),
            vmem((SEQ, HS), BF),
            vmem((SEQ, HS), BF),
            vmem((SEQ, HS), F32),
            vmem((SEQ, HS), F32),
            vmem((SEQ, 2 * HS), BF),
            vmem((D, 2 * HS), F32),
            vmem((D, 2 * HS), BF),
            vmem((D, 2 * HS), BF),
            vmem((D, HS), BF),
            vmem((D, HS), BF),
            vmem((SEQ, SEQ), F32),
            vmem((ROWS, HS), BF),
            vmem((ROWS, HS), BF),
            vmem((16, SEQ), BF),
            vmem((16, SEQ), F32),
            vmem((8, 128), F32),
            vmem((3, 8, 128), F32),
            vmem((8, 128), F32),
            vmem((8, 128), F32),
            vmem((8, 128), F32),
            vmem((8, 128), F32),
            dma((3,)),
            dma((N_IN,)),
            dma((N_IN,)),
            dma((N_IN,)),
            dma((N_IN,)),
            dma,
            dma,
            dma((3,)),
            dma((3,)),
            dma((N_OUT,)),
            dma((N_OUT,)),
            dma,
            dma,
            dma,
            dma,
            dma((2,)),
            dma((2,)),
            pltpu.SemaphoreType.REGULAR,
            dma((2, GROUP)),
            dma((2, N_OUT)),
        ],
        compiler_params=pltpu.CompilerParams(
            collective_id=level, has_side_effects=True, vmem_limit_bytes=58 * MIB
        ),
        cost_estimate=pl.CostEstimate(
            flops=7_000_000_000, bytes_accessed=16 * MIB, transcendentals=2_000_000
        ),
    )(hid, qin, gin, ids, kin, vin, push)


def body(hidden_in, queries, out_grad, token_ids, key_weight, value_weight, push_weight, gossip):
    args = (
        hidden_in[0], queries.reshape(N_BLOCK, BLOCK, GROUP * HS),
        out_grad.reshape(N_BLOCK, BLOCK, GROUP * HS), token_ids, key_weight[0],
        value_weight[0], push_weight.reshape(1, 1),
    )
    new_key, new_value, new_push = lax.switch(
        gossip[0], [partial(run, level) for level in range(LEVELS)], *args
    )
    return new_key[None], new_value[None], new_push.reshape(1)


def solution(mesh):
    return jax.shard_map(
        body,
        mesh=mesh,
        in_specs=(
            P("rep", "tp", None),
            P("rep", None, "tp"),
            P("rep", None, "tp"),
            P("rep", None),
            P("rep", None, "tp"),
            P("rep", None, "tp"),
            P("rep"),
            P(),
        ),
        out_specs=(P("rep", None, "tp"), P("rep", None, "tp"), P("rep")),
        check_vma=False,
    )
```

```python
from functools import partial
import math

import jax
import jax.numpy as jnp
from jax import lax
from jax.experimental import pallas as pl
from jax.experimental.pallas import tpu as pltpu
from jax.sharding import PartitionSpec as P

D = 8192
HS = 128
KVH = 4
GROUP = 8
LEVELS = 3
TOK = 128
SEQ = 512
N_REP = 64

doc_start = 128000
learn_rate = 0.5
epsilon = 1e-06

MESH = pl.DeviceIdType.MESH
BF = jnp.bfloat16
F32 = jnp.float32
MIB = 1024 * 1024

COLS = 256
N_IN = D // COLS
ROWS = 512
N_OUT = D // ROWS
BLOCK = 128
N_BLOCK = SEQ // BLOCK
HALF = SEQ // 2
SPAN = 2
WIDE = 1024


def dot_nn(a, b):
    return lax.dot_general(a, b, (((1,), (0,)), ((), ())), preferred_element_type=F32)


def dot_nt(a, b):
    return lax.dot_general(a, b, (((1,), (1,)), ((), ())), preferred_element_type=F32)


def dot_tn(a, b):
    return lax.dot_general(a, b, (((0,), (0,)), ((), ())), preferred_element_type=F32)


def kernel(
    distance,
    hid, qin, gin, ids, kin, vin, push,
    out_k, out_v, out_push,
    hbuf, qbuf, gbuf, kw, vw, bias, zbuf, acc, krow, vrow, gk, gv, gpair, gw,
    abuf, rbuf, ostk, ostv, gram, kw_peer, vw_peer, starts, seg_row,
    sq_mine, sq_peer, push_mine, push_peer, factor_mine, factor_peer,
    load_sem, y2_send, y2_recv, fw_send, fw_recv, core_send, core_recv,
    sq_send, sq_recv, rep_send, rep_recv, push_send, push_recv,
    factor_send, factor_recv, ahead_send, ahead_recv, credit, head_sem, out_sem,
):
    rep = lax.axis_index("rep")
    tp = lax.axis_index("tp")
    half = tp // 2
    core = lax.rem(tp, 2)
    other_core = (rep, half * 2 + 1 - core)
    other_half = (rep, (1 - half) * 2 + core)
    diagonal = (rep, (1 - half) * 2 + 1 - core)
    target = (lax.rem(rep + distance, N_REP), tp)
    source = (lax.rem(rep + N_REP - distance, N_REP), tp)

    mine = pl.ds(pl.multiple_of(tp * TOK, TOK), TOK)
    theirs = pl.ds(pl.multiple_of(other_half[1] * TOK, TOK), TOK)

    def remote(src, dst, send, recv, device):
        return pltpu.make_async_remote_copy(
            src_ref=src, dst_ref=dst, send_sem=send, recv_sem=recv,
            device_id=device, device_id_type=MESH,
        )

    loads = [
        pltpu.make_async_copy(src, dst, load_sem.at[n])
        for n, (src, dst) in enumerate(
            [(kin, kw), (vin, vw), (hid, hbuf.at[mine])]
        )
    ]
    head_loads = [
        pltpu.make_async_copy(
            src.at[:, :, pl.ds(g * HS, HS)],
            dst.at[:, pl.ds(g * BLOCK, BLOCK), :],
            head_sem.at[n, g],
        )
        for n, (src, dst) in enumerate([(qin, qbuf), (gin, gbuf)])
        for g in range(GROUP)
    ]
    for copy in loads:
        copy.start()

    barrier = pltpu.get_barrier_semaphore()
    for device in (other_core, other_half, diagonal, source):
        pl.semaphore_signal(barrier, inc=1, device_id=device, device_id_type=MESH)
    pl.semaphore_wait(barrier, 4)

    def across(i):
        cols = pl.ds(pl.multiple_of(i * COLS, COLS), COLS)
        return remote(
            hid.at[:, cols], hbuf.at[mine, cols], y2_send.at[i], y2_recv.at[i], other_half
        )

    def onward(i):
        cols = pl.ds(pl.multiple_of(i * COLS, COLS), COLS)
        return remote(
            hbuf.at[theirs, cols], hbuf.at[theirs, cols], fw_send.at[i], fw_recv.at[i], other_core
        )

    def start_across(i, carry):
        across(i).start()
        return carry

    lax.fori_loop(0, N_IN, start_across, 0)
    beside = remote(hid, hbuf.at[mine], core_send, core_recv, other_core)
    beside.start()
    push_f32 = push[0:1, 0:1].astype(F32)
    push_mine[...] = jnp.broadcast_to(push_f32, (8, 128))
    push_along = remote(push_mine, push_peer, push_send, push_recv, target)
    push_along.start()
    for copy in head_loads:
        copy.start()

    with jax.named_scope("mask"):
        starts[...] = jnp.broadcast_to((ids[...] == doc_start).astype(F32), (16, SEQ)).astype(BF)
        seg_row[...] = jnp.zeros_like(seg_row)
        down = lax.broadcasted_iota(jnp.int32, (BLOCK, SEQ), 0)
        over = lax.broadcasted_iota(jnp.int32, (BLOCK, SEQ), 1)

        def add_row(n, carry):
            first = pl.multiple_of(n * BLOCK, BLOCK)
            upper = (down + first <= over).astype(F32).astype(BF)
            seg_row[...] += dot_nn(starts[:, pl.ds(first, BLOCK)], upper)
            return carry

        lax.fori_loop(0, N_BLOCK, add_row, 0)

        def mask_rows(n, carry):
            first = pl.multiple_of(n * BLOCK, BLOCK)
            lower = (over <= down + first).astype(F32).astype(BF)
            seg_col = dot_nt(lower, starts[...])
            allowed = (down + first <= over) & (seg_col[:, 0:1] == seg_row[0:1, :])
            bias[pl.ds(first, BLOCK), :] = jnp.where(allowed, 0.0, -1e30)
            return carry

        lax.fori_loop(0, N_BLOCK, mask_rows, 0)

    acc[...] = jnp.zeros_like(acc)
    gk[...] = jnp.zeros_like(gk)
    gv[...] = jnp.zeros_like(gv)
    gram[...] = jnp.zeros_like(gram)
    inverse = 1.0 / push_f32
    for copy in loads:
        copy.wait()
    beside.wait()

    def project(i, carry):
        @pl.when(i < N_IN)
        def _():
            across(i).wait_recv()
            onward(i).start()

        @pl.when(i > 0)
        def _():
            j = i - 1
            onward(j).wait_recv()
            rows = pl.ds(pl.multiple_of(j * COLS, COLS), COLS)
            zbuf[:, 0:HS] = (kw[rows, :].astype(F32) * inverse).astype(BF)
            zbuf[:, HS:] = (vw[rows, :].astype(F32) * inverse).astype(BF)
            part = hbuf[:, rows]
            acc[...] += dot_nn(part, zbuf[...])
            top, bottom = part[0:HALF, :], part[HALF:, :]
            gram[0:HALF, 0:HALF] += dot_nt(top, top)
            gram[HALF:, :] += dot_nt(bottom, part)

        return carry

    with jax.named_scope("project"):
        lax.fori_loop(0, N_IN + 1, project, 0)

    ahead = [
        remote(src.at[pl.ds(0, ROWS)], dst, ahead_send.at[n], ahead_recv.at[n], target)
        for n, (src, dst) in enumerate([(kin, kw_peer), (vin, vw_peer)])
    ]
    for copy in ahead:
        copy.start()

    scale_model = 1.0 / math.sqrt(D)
    head_scale = 1.0 / math.sqrt(HS)
    krow[...] = (acc[:, 0:HS] * scale_model).astype(BF)
    vrow[...] = (acc[:, HS:] * scale_model).astype(BF)

    for copy in head_loads:
        copy.wait()

    def attend(keys, query, grad, mask):
        scores = dot_nt(krow[0:keys, :], query) * (head_scale * math.log2(math.e))
        scores = scores + jnp.concatenate([mask] * (query.shape[0] // BLOCK), axis=1)
        expo = jnp.exp2(scores - jnp.max(scores, axis=0, keepdims=True))
        grad_p = dot_nt(vrow[0:keys, :], grad)
        prob = expo * (1.0 / jnp.sum(expo, axis=0, keepdims=True))
        prob_bf = prob.astype(BF)
        delta = jnp.sum(prob_bf.astype(F32) * grad_p, axis=0, keepdims=True)
        grad_s = (prob * (grad_p - delta)).astype(BF)
        gv[0:keys, :] += dot_nn(prob_bf, grad)
        gk[0:keys, :] += dot_nn(grad_s, query)

    def attend_step(first, keys, n, carry):
        per_block = GROUP * BLOCK // WIDE
        block = first + n // per_block
        rows = pl.ds(pl.multiple_of(lax.rem(n, per_block) * WIDE, WIDE), WIDE)
        lanes = pl.ds(pl.multiple_of(block * BLOCK, BLOCK), BLOCK)
        attend(keys, qbuf[block, rows, :], gbuf[block, rows, :], bias[0:keys, lanes])
        return carry

    with jax.named_scope("attend"):
        for first in range(0, N_BLOCK, SPAN):
            lax.fori_loop(
                0,
                SPAN * GROUP * BLOCK // WIDE,
                partial(attend_step, first, (first + SPAN) * BLOCK),
                0,
            )
    gpair[:, 0:HS] = (gk[...] * head_scale).astype(BF)
    gpair[:, HS:] = gv[...].astype(BF)

    def weight_grad(i):
        rows = pl.ds(pl.multiple_of(i * ROWS, ROWS), ROWS)
        gw[rows, :] = dot_tn(hbuf[:, rows], gpair[...]) * scale_model

    def along(i):
        rows = pl.ds(pl.multiple_of(i * ROWS, ROWS), ROWS)
        return remote(abuf.at[rows], rbuf.at[rows], rep_send.at[i], rep_recv.at[i], target)

    shares = [
        remote(sq_mine, sq_peer.at[n], sq_send.at[n], sq_recv.at[n], device)
        for n, device in enumerate((other_core, other_half, diagonal))
    ]
    factor_along = remote(factor_mine, factor_peer, factor_send, factor_recv, target)

    def share_squares():
        def add_rows(n, total):
            rows = pl.ds(pl.multiple_of(n * HALF, HALF), HALF)
            pair = gpair[...]
            column = lax.broadcasted_iota(jnp.int32, (HALF, SEQ), 1)
            whole = gram[rows, :] * jnp.where(column < n * HALF, 2.0, 1.0)
            high = whole.astype(BF)
            rest = whole - high.astype(F32)
            middle = rest.astype(BF)
            low = (rest - middle.astype(F32)).astype(BF)
            spread = dot_nn(low, pair) + dot_nn(middle, pair) + dot_nn(high, pair)
            return total + jnp.sum(spread * gpair[rows, :].astype(F32), axis=0, keepdims=True)

        total = lax.fori_loop(0, SEQ // HALF, add_rows, jnp.zeros((1, 2 * HS), F32))
        total = jnp.maximum(jnp.sum(total, keepdims=True), 0.0) * (scale_model * scale_model)
        sq_mine[...] = jnp.broadcast_to(total, (8, 128))
        for copy in shares:
            copy.start()

    def settle_factor():
        push_along.wait()
        for copy in shares:
            copy.wait()
        squares = (sq_mine[...] + sq_peer[0]) + (sq_peer[1] + sq_peer[2])
        factor_mine[...] = lax.rsqrt(squares / (2 * D * KVH * HS) + epsilon)
        pl.semaphore_signal(credit, inc=1, device_id=source, device_id_type=MESH)
        factor_along.start()
        pl.semaphore_wait(credit, 1)

    def own_part(rows):
        step = (gw[rows, :] * factor_mine[0:1, 0:1]).astype(BF).astype(F32)
        own_k = 0.5 * kw[rows, :].astype(F32) - (0.5 * learn_rate) * step[:, 0:HS]
        own_v = 0.5 * vw[rows, :].astype(F32) - (0.5 * learn_rate) * step[:, HS:]
        return own_k, own_v

    def send_part(i, carry):
        rows = pl.ds(pl.multiple_of(i * ROWS, ROWS), ROWS)
        weight_grad(i)

        @pl.when(i == 0)
        def _():
            abuf[rows, :] = gw[rows, :].astype(BF)
            along(i).start()
            share_squares()

        @pl.when(i == 1)
        def _():
            settle_factor()

        @pl.when(i > 0)
        def _():
            own_k, own_v = own_part(rows)
            abuf[rows, 0:HS] = own_k.astype(BF)
            abuf[rows, HS:] = own_v.astype(BF)
            along(i).start()

        return carry

    with jax.named_scope("send_parts"):
        lax.fori_loop(0, N_OUT, send_part, 0)

    out_push[...] = (0.5 * (push_f32 + push_peer[0:1, 0:1])).astype(BF)

    def written(i):
        rows = pl.ds(pl.multiple_of(i * ROWS, ROWS), ROWS)
        return (
            pltpu.make_async_copy(ostk.at[rows], out_k.at[rows], out_sem.at[0, i]),
            pltpu.make_async_copy(ostv.at[rows], out_v.at[rows], out_sem.at[1, i]),
        )

    def mix(i, carry):
        rows = pl.ds(pl.multiple_of(i * ROWS, ROWS), ROWS)
        own_k, own_v = own_part(rows)
        along(i).wait_recv()

        @pl.when(i == 0)
        def _():
            step = (rbuf[rows, :].astype(F32) * factor_peer[0:1, 0:1]).astype(BF).astype(F32)
            peer_k = 0.5 * kw_peer[...].astype(F32) - (0.5 * learn_rate) * step[:, 0:HS]
            peer_v = 0.5 * vw_peer[...].astype(F32) - (0.5 * learn_rate) * step[:, HS:]
            ostk[rows, :] = (own_k + peer_k).astype(BF)
            ostv[rows, :] = (own_v + peer_v).astype(BF)

        @pl.when(i > 0)
        def _():
            ostk[rows, :] = (own_k + rbuf[rows, 0:HS].astype(F32)).astype(BF)
            ostv[rows, :] = (own_v + rbuf[rows, HS:].astype(F32)).astype(BF)

        for copy in written(i):
            copy.start()
        return carry

    factor_along.wait()
    for copy in ahead:
        copy.wait()
    with jax.named_scope("mix"):
        lax.fori_loop(0, N_OUT, mix, 0)

    def finish(i, carry):
        along(i).wait_send()
        for copy in written(i):
            copy.wait()
        return carry

    lax.fori_loop(0, N_OUT, finish, 0)

    def sent(i, carry):
        across(i).wait_send()
        onward(i).wait_send()
        return carry

    lax.fori_loop(0, N_IN, sent, 0)


def run(level, hid, qin, gin, ids, kin, vin, push):
    vmem = pltpu.VMEM
    dma = pltpu.SemaphoreType.DMA
    whole = pl.BlockSpec(memory_space=pltpu.VMEM)
    hbm = pl.BlockSpec(memory_space=pl.ANY)
    return pl.pallas_call(
        partial(kernel, 1 << level),
        name=f"gossip_step_{1 << level}",
        out_shape=(
            jax.ShapeDtypeStruct((D, HS), BF),
            jax.ShapeDtypeStruct((D, HS), BF),
            jax.ShapeDtypeStruct((1, 1), BF),
        ),
        in_specs=[hbm, hbm, hbm, whole, hbm, hbm, whole],
        out_specs=(hbm, hbm, whole),
        scratch_shapes=[
            vmem((SEQ, D), BF),
            vmem((N_BLOCK, GROUP * BLOCK, HS), BF),
            vmem((N_BLOCK, GROUP * BLOCK, HS), BF),
            vmem((D, HS), BF),
            vmem((D, HS), BF),
            vmem((SEQ, SEQ), F32),
            vmem((COLS, 2 * HS), BF),
            vmem((SEQ, 2 * HS), F32),
            vmem((SEQ, HS), BF),
            vmem((SEQ, HS), BF),
            vmem((SEQ, HS), F32),
            vmem((SEQ, HS), F32),
            vmem((SEQ, 2 * HS), BF),
            vmem((D, 2 * HS), F32),
            vmem((D, 2 * HS), BF),
            vmem((D, 2 * HS), BF),
            vmem((D, HS), BF),
            vmem((D, HS), BF),
            vmem((SEQ, SEQ), F32),
            vmem((ROWS, HS), BF),
            vmem((ROWS, HS), BF),
            vmem((16, SEQ), BF),
            vmem((16, SEQ), F32),
            vmem((8, 128), F32),
            vmem((3, 8, 128), F32),
            vmem((8, 128), F32),
            vmem((8, 128), F32),
            vmem((8, 128), F32),
            vmem((8, 128), F32),
            dma((3,)),
            dma((N_IN,)),
            dma((N_IN,)),
            dma((N_IN,)),
            dma((N_IN,)),
            dma,
            dma,
            dma((3,)),
            dma((3,)),
            dma((N_OUT,)),
            dma((N_OUT,)),
            dma,
            dma,
            dma,
            dma,
            dma((2,)),
            dma((2,)),
            pltpu.SemaphoreType.REGULAR,
            dma((2, GROUP)),
            dma((2, N_OUT)),
        ],
        compiler_params=pltpu.CompilerParams(
            collective_id=level, has_side_effects=True, vmem_limit_bytes=58 * MIB
        ),
        cost_estimate=pl.CostEstimate(
            flops=7_000_000_000, bytes_accessed=16 * MIB, transcendentals=2_000_000
        ),
    )(hid, qin, gin, ids, kin, vin, push)


def body(hidden_in, queries, out_grad, token_ids, key_weight, value_weight, push_weight, gossip):
    args = (
        hidden_in[0], queries.reshape(N_BLOCK, BLOCK, GROUP * HS),
        out_grad.reshape(N_BLOCK, BLOCK, GROUP * HS), token_ids, key_weight[0],
        value_weight[0], push_weight.reshape(1, 1),
    )
    new_key, new_value, new_push = lax.switch(
        gossip[0], [partial(run, level) for level in range(LEVELS)], *args
    )
    return new_key[None], new_value[None], new_push.reshape(1)


def solution(mesh):
    return jax.shard_map(
        body,
        mesh=mesh,
        in_specs=(
            P("rep", "tp", None),
            P("rep", None, "tp"),
            P("rep", None, "tp"),
            P("rep", None),
            P("rep", None, "tp"),
            P("rep", None, "tp"),
            P("rep"),
            P(),
        ),
        out_specs=(P("rep", None, "tp"), P("rep", None, "tp"), P("rep")),
        check_vma=False,
    )
```
